32 devices in a mesh: row: 8 (over y, x, core), col: 4 (over z).
Axes of the slice: x: 2, y: 2, z: 4, core: 2. Of those that a mesh axis runs over, the one named last changes fastest.
Arguments:
- traces: bfloat16 [4096, 782], P(('row', 'col')), may hold values from -60 to 60
- taps: float32 [16], replicated, may hold values from -1.5 to 1.5
Outputs:
- correlations: float32 [32, 4096, 4096], P(None, 'row', 'col')
The draws below stay inside these ranges and needn't reach their ends.
All inputs are finite; a program needn't handle non-finite values.
Results may differ from the reference program's by a relative error of at most 0.0036.
Values may be sent and summed in bfloat16 or wider, within the bound.
A program may use at most 256 MiB of HBM per device.

```python
import math
import jax
import jax.numpy as jnp
from jax import lax

C = 4096
TAPS = 16
LAGS = 32
M = 384
SR = 782
W = 353


def draw_traces(key, part):
    first, second = jax.random.split(key, 2)
    scales = jnp.exp(jax.random.uniform(first, (C, 1), jnp.float32, 0.0, math.log(10.0)))
    noise = jnp.clip(jax.random.normal(second, (C, SR), jnp.float32), -5.0, 5.0)
    values = scales * noise
    return values.astype(jnp.bfloat16)


def scatter_about(stream_key, shape, scale, limit, kind=jnp.bfloat16):
    drawn = scale * jax.random.normal(stream_key, shape, jnp.float32)
    return jnp.clip(drawn, min=-limit, max=limit).astype(kind)


def setup_inputs(seed: int = 0) -> dict:
    seeds = jax.random.split(jax.random.key(seed), 3)
    return {
        "traces": draw_traces(jax.random.fold_in(seeds[2], 71), 0),
        "taps": scatter_about(seeds[1], (TAPS,), TAPS ** -0.5, 1.5, jnp.float32),
    }


def whiten(traces, taps):
    samples = traces.astype(jnp.float32)
    decimated = jnp.zeros((samples.shape[0], M), jnp.float32)
    for k in range(TAPS):
        decimated = decimated + taps[k] * samples[:, k:k + 2 * M - 1:2]
    centred = decimated - lax.optimization_barrier(jnp.mean(decimated, axis=1, keepdims=True))
    spread = jnp.sqrt(lax.optimization_barrier(jnp.mean(centred * centred, axis=1, keepdims=True)) + 1e-06)
    return (centred / spread).astype(jnp.bfloat16)

def reference(traces, taps):
    whitened = whiten(traces, taps).astype(jnp.float32)
    left = whitened[:, :W]
    factor = 1.0 / math.sqrt(W)

    def one_lag(lag):
        right = lax.dynamic_slice_in_dim(whitened, lag, W, 1)
        return jnp.dot(left, right.T, precision=lax.Precision.HIGHEST, preferred_element_type=jnp.float32) * factor
    return lax.map(one_lag, jnp.arange(LAGS, dtype=jnp.int32))
```

```python
import functools
import math

import jax
import jax.numpy as jnp
from jax import lax
from jax.experimental import pallas as pl
from jax.experimental.pallas import tpu as pltpu
from jax.sharding import PartitionSpec as P

LAGS = 32
MESH = pl.DeviceIdType.MESH


def whiten(x_ref, taps_ref, count):
    taps = taps_ref.shape[0]
    tile = 128
    depth = 2 * tile + taps - 2
    m = lax.broadcasted_iota(jnp.int32, (depth, tile), 0)
    n = lax.broadcasted_iota(jnp.int32, (depth, tile), 1)
    offset = m - 2 * n
    band = jnp.zeros((depth, tile), jnp.float32)
    for k in range(taps):
        band = jnp.where(offset == k, taps_ref[k], band)
    high = band.astype(jnp.bfloat16)
    rest = band - high.astype(jnp.float32)
    middle = rest.astype(jnp.bfloat16)
    low = (rest - middle.astype(jnp.float32)).astype(jnp.bfloat16)
    pieces = []
    for t in range(count // tile):
        x = x_ref[:, 2 * tile * t : 2 * tile * t + depth]
        total = jnp.dot(x, low, preferred_element_type=jnp.float32)
        total += jnp.dot(x, middle, preferred_element_type=jnp.float32)
        total += jnp.dot(x, high, preferred_element_type=jnp.float32)
        pieces.append(total)
    decimated = jnp.concatenate(pieces, axis=1)
    centred = decimated - jnp.mean(decimated, axis=1, keepdims=True)
    spread = jnp.sqrt(jnp.mean(centred * centred, axis=1, keepdims=True) + 1e-06)
    return (centred / spread).astype(jnp.bfloat16)


def gather_kernel(R, C, count, x_ref, taps_ref, first, second, send1, recv1, send2, recv2, sendp, recvp):
    r = lax.axis_index("row")
    c = lax.axis_index("col")
    block = r * C + c
    to_r, to_c = lax.rem(block, R), lax.div(block, R)
    wanted = c * R + r
    from_r, from_c = lax.div(wanted, C), lax.rem(wanted, C)
    fixed = wanted == block

    barrier = pltpu.get_barrier_semaphore()

    def greet(row, col):
        pl.semaphore_signal(barrier, inc=1, device_id=(row, col), device_id_type=MESH)

    for k in range(1, R):
        greet(lax.rem(r + k, R), c)
    for k in range(1, C):
        greet(r, lax.rem(c + k, C))

    @pl.when(jnp.logical_not(fixed))
    def _():
        greet(to_r, to_c)
        greet(from_r, from_c)

    mine = whiten(x_ref, taps_ref, count)
    first[pl.ds(c, 1)] = mine[None]

    @pl.when(fixed)
    def _():
        second[pl.ds(r, 1)] = mine[None]

    pl.semaphore_wait(barrier, R - 1 + C - 1 + jnp.where(fixed, 0, 2))

    def swap():
        return pltpu.make_async_remote_copy(
            first.at[c], second.at[to_r], sendp, recvp, device_id=(to_r, to_c), device_id_type=MESH)

    def arrived_swap():
        return pltpu.make_async_remote_copy(
            first.at[c], second.at[r], sendp, recvp, device_id=(to_r, to_c), device_id_type=MESH)

    def col_copy(slot, col, way):
        return pltpu.make_async_remote_copy(
            first.at[slot], first.at[slot], send1.at[way, slot], recv1.at[slot],
            device_id=(r, col), device_id_type=MESH)

    def row_copy(slot, row, k):
        return pltpu.make_async_remote_copy(
            second.at[slot], second.at[slot], send2.at[k], recv2.at[slot],
            device_id=(row, c), device_id_type=MESH)

    @pl.when(jnp.logical_not(fixed))
    def _():
        swap().start()

    @pl.when(c + 1 < C)
    def _():
        col_copy(c, c + 1, 0).start()

    @pl.when(c >= 1)
    def _():
        col_copy(c, c - 1, 1).start()

    @pl.when(jnp.logical_not(fixed))
    def _():
        arrived_swap().wait_recv()

    half = R // 2
    core = lax.rem(r, 2)
    chip = lax.div(r, 2)
    partner = r + 1 - 2 * core
    for k in list(range(1, half)):
        row_copy(r, 2 * lax.rem(chip + k, half) + core, k).start()
    row_copy(r, partner, 0).start()

    for step in range(1, max(half, C)):
        if step < C:
            left, right = c - step, c + step

            @pl.when(left >= 0)
            def _():
                col_copy(left, c, 0).wait_recv()

                @pl.when(c + 1 < C)
                def _():
                    col_copy(left, c + 1, 0).start()

            @pl.when(right < C)
            def _():
                col_copy(right, c, 1).wait_recv()

                @pl.when(c >= 1)
                def _():
                    col_copy(right, c - 1, 1).start()

        if step < half:
            slot = 2 * lax.rem(chip + half - step, half) + core
            row_copy(slot, partner, 0).wait_recv()
            row_copy(slot, partner, half + step).start()

    for k in range(half):
        slot = 2 * lax.rem(chip + k, half) + 1 - core
        row_copy(slot, partner, 0).wait_recv()

    for k in range(half):
        row_copy(r, partner, k).wait_send()
    for k in range(1, half):
        row_copy(r, partner, half + k).wait_send()

    @pl.when(jnp.logical_not(fixed))
    def _():
        swap().wait_send()

    for slot in range(C):
        @pl.when(jnp.logical_and(slot <= c, c + 1 < C))
        def _():
            col_copy(slot, c + 1, 0).wait_send()

        @pl.when(jnp.logical_and(slot >= c, c >= 1))
        def _():
            col_copy(slot, c - 1, 1).wait_send()


def gather(R, C, count, traces, taps):
    rows = traces.shape[0]
    vmem = pl.BlockSpec(memory_space=pltpu.VMEM)
    return pl.pallas_call(
        functools.partial(gather_kernel, R, C, count),
        out_shape=(
            jax.ShapeDtypeStruct((C, rows, count), jnp.bfloat16),
            jax.ShapeDtypeStruct((R, rows, count), jnp.bfloat16),
        ),
        in_specs=[vmem, pl.BlockSpec(memory_space=pltpu.SMEM)],
        out_specs=(vmem, vmem),
        scratch_shapes=[
            pltpu.SemaphoreType.DMA((2, C)),
            pltpu.SemaphoreType.DMA((C,)),
            pltpu.SemaphoreType.DMA((R,)),
            pltpu.SemaphoreType.DMA((R,)),
            pltpu.SemaphoreType.DMA,
            pltpu.SemaphoreType.DMA,
        ],
        compiler_params=pltpu.CompilerParams(
            collective_id=0, has_side_effects=True, vmem_limit_bytes=32 * 1024 * 1024),
        name="whiten_gather",
    )(traces, taps)


def correlate_kernel(width, per_step, first, second, out, left, right, lagged):
    rows = left.shape[0]

    @pl.when(pl.program_id(0) == 0)
    def _():
        n = lax.broadcasted_iota(jnp.int32, left.shape, 1)
        left[...] = jnp.where(n < width, first[...].astype(jnp.float32), 0.0)
        right[...] = second[...].T

    scale = 1.0 / math.sqrt(width)
    x = left[...]
    for k in range(per_step):
        lagged[k * rows : (k + 1) * rows] = x.astype(jnp.bfloat16)
        x = pltpu.roll(x, 1, 1)
    left[...] = x
    product = jnp.dot(lagged[...], right[...], preferred_element_type=jnp.float32) * scale
    out[...] = product.reshape(out.shape)


def correlate(first, second, width, per_step=4):
    rows, count = first.shape
    columns = second.shape[0]
    return pl.pallas_call(
        functools.partial(correlate_kernel, width, per_step),
        out_shape=jax.ShapeDtypeStruct((LAGS, rows, columns), jnp.float32),
        grid=(LAGS // per_step,),
        in_specs=[
            pl.BlockSpec((rows, count), lambda s: (0, 0)),
            pl.BlockSpec((columns, count), lambda s: (0, 0)),
        ],
        out_specs=pl.BlockSpec((per_step, rows, columns), lambda s: (s, 0, 0)),
        scratch_shapes=[
            pltpu.VMEM((rows, count), jnp.float32),
            pltpu.VMEM((count, columns), jnp.bfloat16),
            pltpu.VMEM((per_step * rows, count), jnp.bfloat16),
        ],
        compiler_params=pltpu.CompilerParams(vmem_limit_bytes=48 * 1024 * 1024),
        cost_estimate=pl.CostEstimate(
            flops=2 * LAGS * rows * columns * count,
            bytes_accessed=4 * LAGS * rows * columns, transcendentals=0),
        name="correlate",
    )(first, second)


def solution(mesh):
    R, C = mesh.shape["row"], mesh.shape["col"]

    def on_device(traces, taps):
        count = (traces.shape[1] - taps.shape[0] + 2) // 2
        width = count - LAGS + 1
        first, second = gather(R, C, count, traces, taps)
        first = first.reshape(-1, count)
        second = second.reshape(-1, count)
        return correlate(first, second, width)

    placed = (P(("row", "col"), None), P())
    return jax.shard_map(
        on_device, mesh=mesh, in_specs=placed, out_specs=P(None, "row", "col"), check_vma=False
    )
```

```python
import functools
import math

import jax
import jax.numpy as jnp
from jax import lax
from jax.experimental import pallas as pl
from jax.experimental.pallas import tpu as pltpu
from jax.sharding import PartitionSpec as P

LAGS = 32
MESH = pl.DeviceIdType.MESH


def whiten(x_ref, taps_ref, count):
    taps = taps_ref.shape[0]
    tile = 128
    depth = 2 * tile + taps - 2
    m = lax.broadcasted_iota(jnp.int32, (depth, tile), 0)
    n = lax.broadcasted_iota(jnp.int32, (depth, tile), 1)
    offset = m - 2 * n
    band = jnp.zeros((depth, tile), jnp.float32)
    for k in range(taps):
        band = jnp.where(offset == k, taps_ref[k], band)
    high = band.astype(jnp.bfloat16)
    rest = band - high.astype(jnp.float32)
    middle = rest.astype(jnp.bfloat16)
    low = (rest - middle.astype(jnp.float32)).astype(jnp.bfloat16)
    over_samples = (((0,), (0,)), ((), ()))
    pieces = []
    for t in range(count // tile):
        x = x_ref[2 * tile * t : 2 * tile * t + depth]
        total = lax.dot_general(x, low, over_samples, preferred_element_type=jnp.float32)
        total += lax.dot_general(x, middle, over_samples, preferred_element_type=jnp.float32)
        total += lax.dot_general(x, high, over_samples, preferred_element_type=jnp.float32)
        pieces.append(total)
    decimated = jnp.concatenate(pieces, axis=1)
    centred = decimated - jnp.mean(decimated, axis=1, keepdims=True)
    spread = jnp.sqrt(jnp.mean(centred * centred, axis=1, keepdims=True) + 1e-06)
    return (centred / spread).astype(jnp.bfloat16)


def gather_kernel(R, C, count, x_ref, taps_ref, first, second, send1, recv1, send2, recv2, sendp, recvp):
    r = lax.axis_index("row")
    c = lax.axis_index("col")
    block = r * C + c
    to_r, to_c = lax.rem(block, R), lax.div(block, R)
    wanted = c * R + r
    from_r, from_c = lax.div(wanted, C), lax.rem(wanted, C)
    fixed = wanted == block

    barrier = pltpu.get_barrier_semaphore()

    def greet(row, col):
        pl.semaphore_signal(barrier, inc=1, device_id=(row, col), device_id_type=MESH)

    for k in range(1, R):
        greet(lax.rem(r + k, R), c)
    for k in range(1, C):
        greet(r, lax.rem(c + k, C))

    @pl.when(jnp.logical_not(fixed))
    def _():
        greet(to_r, to_c)
        greet(from_r, from_c)

    mine = whiten(x_ref, taps_ref, count)
    first[pl.ds(c, 1)] = mine[None]

    @pl.when(fixed)
    def _():
        second[pl.ds(r, 1)] = mine[None]

    pl.semaphore_wait(barrier, R - 1 + C - 1 + jnp.where(fixed, 0, 2))

    def swap():
        return pltpu.make_async_remote_copy(
            first.at[c], second.at[to_r], sendp, recvp, device_id=(to_r, to_c), device_id_type=MESH)

    def arrived_swap():
        return pltpu.make_async_remote_copy(
            first.at[c], second.at[r], sendp, recvp, device_id=(to_r, to_c), device_id_type=MESH)

    def col_copy(slot, col, way):
        return pltpu.make_async_remote_copy(
            first.at[slot], first.at[slot], send1.at[way, slot], recv1.at[slot],
            device_id=(r, col), device_id_type=MESH)

    def row_copy(slot, row, k):
        return pltpu.make_async_remote_copy(
            second.at[slot], second.at[slot], send2.at[k], recv2.at[slot],
            device_id=(row, c), device_id_type=MESH)

    @pl.when(jnp.logical_not(fixed))
    def _():
        swap().start()

    @pl.when(c + 1 < C)
    def _():
        col_copy(c, c + 1, 0).start()

    @pl.when(c >= 1)
    def _():
        col_copy(c, c - 1, 1).start()

    @pl.when(jnp.logical_not(fixed))
    def _():
        arrived_swap().wait_recv()

    half = R // 2
    core = lax.rem(r, 2)
    chip = lax.div(r, 2)
    partner = r + 1 - 2 * core
    for k in list(range(1, half)):
        row_copy(r, 2 * lax.rem(chip + k, half) + core, k).start()
    row_copy(r, partner, 0).start()

    for step in range(1, C):
        left, right = c - step, c + step

        @pl.when(left >= 0)
        def _():
            col_copy(left, c, 0).wait_recv()

            @pl.when(c + 1 < C)
            def _():
                col_copy(left, c + 1, 0).start()

        @pl.when(right < C)
        def _():
            col_copy(right, c, 1).wait_recv()

            @pl.when(c >= 1)
            def _():
                col_copy(right, c - 1, 1).start()

    for step in range(1, half):
        slot = 2 * lax.rem(chip + half - step, half) + core
        row_copy(slot, partner, 0).wait_recv()
        row_copy(slot, partner, half + step).start()

    for k in range(half):
        slot = 2 * lax.rem(chip + k, half) + 1 - core
        row_copy(slot, partner, 0).wait_recv()

    for k in range(half):
        row_copy(r, partner, k).wait_send()
    for k in range(1, half):
        row_copy(r, partner, half + k).wait_send()

    @pl.when(jnp.logical_not(fixed))
    def _():
        swap().wait_send()

    for slot in range(C):
        @pl.when(jnp.logical_and(slot <= c, c + 1 < C))
        def _():
            col_copy(slot, c + 1, 0).wait_send()

        @pl.when(jnp.logical_and(slot >= c, c >= 1))
        def _():
            col_copy(slot, c - 1, 1).wait_send()


def gather(R, C, count, traces, taps):
    rows = traces.shape[1]
    vmem = pl.BlockSpec(memory_space=pltpu.VMEM)
    return pl.pallas_call(
        functools.partial(gather_kernel, R, C, count),
        out_shape=(
            jax.ShapeDtypeStruct((C, rows, count), jnp.bfloat16),
            jax.ShapeDtypeStruct((R, rows, count), jnp.bfloat16),
        ),
        in_specs=[vmem, pl.BlockSpec(memory_space=pltpu.SMEM)],
        out_specs=(vmem, vmem),
        scratch_shapes=[
            pltpu.SemaphoreType.DMA((2, C)),
            pltpu.SemaphoreType.DMA((C,)),
            pltpu.SemaphoreType.DMA((R,)),
            pltpu.SemaphoreType.DMA((R,)),
            pltpu.SemaphoreType.DMA,
            pltpu.SemaphoreType.DMA,
        ],
        compiler_params=pltpu.CompilerParams(
            collective_id=0, has_side_effects=True, vmem_limit_bytes=32 * 1024 * 1024),
        name="whiten_gather",
    )(traces, taps)


def correlate_kernel(width, per_step, first, second, out, left, right, lagged):
    rows = left.shape[0]

    @pl.when(pl.program_id(0) == 0)
    def _():
        n = lax.broadcasted_iota(jnp.int32, left.shape, 1)
        left[...] = jnp.where(n < width, first[...].astype(jnp.float32), 0.0)
        right[...] = second[...].T

    scale = 1.0 / math.sqrt(width)
    x = left[...]
    for k in range(per_step):
        lagged[k * rows : (k + 1) * rows] = x.astype(jnp.bfloat16)
        x = pltpu.roll(x, 1, 1)
    left[...] = x
    product = jnp.dot(lagged[...], right[...], preferred_element_type=jnp.float32) * scale
    out[...] = product.reshape(out.shape)


def correlate(first, second, width, per_step=4):
    rows, count = first.shape
    columns = second.shape[0]
    return pl.pallas_call(
        functools.partial(correlate_kernel, width, per_step),
        out_shape=jax.ShapeDtypeStruct((LAGS, rows, columns), jnp.float32),
        grid=(LAGS // per_step,),
        in_specs=[
            pl.BlockSpec((rows, count), lambda s: (0, 0)),
            pl.BlockSpec((columns, count), lambda s: (0, 0)),
        ],
        out_specs=pl.BlockSpec((per_step, rows, columns), lambda s: (s, 0, 0)),
        scratch_shapes=[
            pltpu.VMEM((rows, count), jnp.float32),
            pltpu.VMEM((count, columns), jnp.bfloat16),
            pltpu.VMEM((per_step * rows, count), jnp.bfloat16),
        ],
        compiler_params=pltpu.CompilerParams(vmem_limit_bytes=48 * 1024 * 1024),
        cost_estimate=pl.CostEstimate(
            flops=2 * LAGS * rows * columns * count,
            bytes_accessed=4 * LAGS * rows * columns, transcendentals=0),
        name="correlate",
    )(first, second)


def solution(mesh):
    R, C = mesh.shape["row"], mesh.shape["col"]

    def on_device(traces, taps):
        count = (traces.shape[1] - taps.shape[0] + 2) // 2
        width = count - LAGS + 1
        first, second = gather(R, C, count, traces.T, taps)
        first = first.reshape(-1, count)
        second = second.reshape(-1, count)
        return correlate(first, second, width)

    placed = (P(("row", "col"), None), P())
    return jax.shard_map(
        on_device, mesh=mesh, in_specs=placed, out_specs=P(None, "row", "col"), check_vma=False
    )
```
